512 devices in a mesh: sec: 16 (over z_hi, y, core), xy: 32 (over z_lo, x).
Axes of the slice: x: 4, y: 4, z: 16 (z_hi: 2, z_lo: 8; z = z_hi * 8 + z_lo), core: 2. Of those that a mesh axis runs over, the one named last changes fastest.
Arguments:
- image: bfloat16 [16, 4096, 512], P('sec', 'xy'), may hold values from -11 to 11
- mask: int32 [16, 4096, 512], P('sec', 'xy'), may hold values from 0 to 1
- flags: int32 [16, 32, 4], P('sec', 'xy'), may hold values 0 or 1
Outputs:
- scores: float32 [16, 32, 4, 1089], P('sec', 'xy')
The draws below stay inside these ranges and needn't reach their ends.
All inputs are finite; a program needn't handle non-finite values. No bound on the sum of `flags` on one device may be relied on, other than what follows from the above.
Results may differ from the reference program's by a relative error of at most 0.0025.
Values may be sent and summed in bfloat16 or wider, within the bound.
No kernel may reach another device: no remote copies, remote signals or barrier semaphores. Data moves between devices by JAX's collectives and lax.ppermute only.
A program may use at most 64 MiB of HBM per device.

```python
import jax
import jax.numpy as jnp
from jax import lax

PATCH = 128
SEARCH = 16
BOX = 8
PCOL = 4
SECTIONS = 16
NPROW = 32
NY = 4096
W = 512
SPAN = 33
DISP = 1089


def draw_image(key, part):
    key = jax.random.fold_in(key, 11)
    k_rows, k_cols, k_base, k_noise = jax.random.split(key, 4)
    half_step = SEARCH // 2
    margin = SECTIONS * SEARCH
    row_offsets = jnp.cumsum(jax.random.randint(k_rows, (SECTIONS,), -half_step, half_step + 1)) + SECTIONS * half_step
    col_offsets = jnp.cumsum(jax.random.randint(k_cols, (SECTIONS,), -half_step, half_step + 1)) + SECTIONS * half_step
    base_field = jax.random.truncated_normal(k_base, -4.0, 4.0, (NY + margin, W + margin), jnp.float32)
    noise_field = jax.random.truncated_normal(k_noise, -4.0, 4.0, (SECTIONS, NY, W), jnp.float32)
    frames = jax.vmap(lambda row_start, col_start: lax.dynamic_slice(base_field, (row_start, col_start), (NY, W)))(row_offsets, col_offsets)
    return (0.8 * frames + 0.6 * noise_field).astype(jnp.bfloat16)


def draw_mask(key, part):
    key = jax.random.fold_in(key, 12)
    k_level, k_pixel = jax.random.split(key, 2)
    block_len = PATCH // 2
    levels = jax.random.randint(k_level, (SECTIONS, NY // block_len, W // block_len), 0, 5)
    level_map = jnp.repeat(jnp.repeat(levels, block_len, axis=1), block_len, axis=2)
    pixels = jax.random.randint(k_pixel, (SECTIONS, NY, W), 0, 4)
    return (pixels < level_map).astype(jnp.int32)


def place_ends(entries, own_key, low, top_value):
    longest = entries.shape.index(max(entries.shape))
    spots = []
    for shift in (0, 1):
        where = [jax.random.randint(jax.random.fold_in(own_key, axis), (), 0, length) for axis, length in enumerate(entries.shape)]
        where[longest] = (where[longest] + shift) % entries.shape[longest]
        spots.append(tuple(where))
    return entries.at[spots[0]].set(low).at[spots[1]].set(top_value)


def setup_inputs(seed: int = 0) -> dict:
    key_of = jax.random.split(jax.random.key(seed), 4)
    image = draw_image(jax.random.fold_in(key_of[3], 71), 0)
    mask = draw_mask(jax.random.fold_in(key_of[3], 71), 0)
    flags = place_ends((jax.random.randint(key_of[2], (SECTIONS, NPROW, PCOL), 0, 8) < 7).astype(jnp.int32), jax.random.fold_in(key_of[2], 1), 0, 1)
    return dict(image=image, mask=mask, flags=flags)


FLOOR_SHARE = 0.25
EPSILON = 1e-05

def window_sum(values, along_dim, window_len, out_count):
    running = jnp.cumsum(values, axis=along_dim)
    zero_row = jnp.zeros_like(lax.slice_in_dim(values, 0, 1, axis=along_dim))
    running = jnp.concatenate([zero_row, running], axis=along_dim)
    upper = lax.slice_in_dim(running, window_len, window_len + out_count, axis=along_dim)
    lower = lax.slice_in_dim(running, 0, out_count, axis=along_dim)
    return upper - lower

def normalize(raw_padded, tissue, box_half):
    row_count, col_count = tissue.shape
    padded = jnp.pad(raw_padded, ((0, 0), (box_half, box_half)))
    side_len = 2 * box_half + 1

    def local_average(values):
        across_sum = window_sum(values, 1, side_len, col_count)
        return window_sum(across_sum, 0, side_len, row_count) / float(side_len * side_len)
    local_mean = local_average(padded)
    local_square = local_average(padded * padded)
    centre = raw_padded[box_half:box_half + row_count]
    scaled = (centre - local_mean) * lax.rsqrt(local_square - local_mean * local_mean + EPSILON)
    return (tissue.astype(jnp.float32) * scaled).astype(jnp.bfloat16)

def windows_of(extended, patch_len, col_count, span_len):
    widened = jnp.pad(extended, ((0, 0), (0, patch_len - span_len + 1)))
    main_part = widened[:, :col_count * patch_len].reshape(-1, col_count, patch_len)
    tail_part = widened[:, patch_len:(col_count + 1) * patch_len].reshape(-1, col_count, patch_len)[:, :, :span_len - 1]
    return jnp.concatenate([main_part, tail_part], axis=2)

def shear_sum(product, span_len):
    lead_shape = product.shape[:-2]
    patch_len = product.shape[-2]
    wide_len = product.shape[-1]
    flattened = product.reshape(lead_shape + (patch_len * wide_len,))
    flattened = jnp.pad(flattened, [(0, 0)] * len(lead_shape) + [(0, patch_len)])
    sheared = flattened.reshape(lead_shape + (patch_len, wide_len + 1))
    return lax.optimization_barrier(jnp.sum(sheared[..., :span_len], axis=-2))

def strip_scores(own_strip, extended, validity):
    patch_len = PATCH
    col_count = PCOL
    span_len = SPAN
    patches = own_strip.astype(jnp.float32).reshape(patch_len, col_count, patch_len)
    windows = windows_of(extended, patch_len, col_count, span_len).astype(jnp.float32)

    def one_shift(shift_index):
        slab_rows = lax.dynamic_slice_in_dim(windows, shift_index.astype(jnp.int32), patch_len, 0)
        product = jnp.einsum('ypx,ypc->pxc', patches, slab_rows, precision=lax.Precision.HIGHEST)
        return shear_sum(product, span_len)
    numerator = lax.map(one_shift, jnp.arange(span_len, dtype=jnp.int32))
    squares = windows * windows
    energy_next = window_sum(window_sum(squares, 0, patch_len, span_len), 2, patch_len, span_len)
    energy_own = lax.optimization_barrier(jnp.sum(patches * patches, axis=(0, 2)))
    floor_value = FLOOR_SHARE * patch_len * patch_len
    denominator = jnp.sqrt(jnp.maximum(energy_own, floor_value)[None, :, None] * jnp.maximum(energy_next, floor_value))
    ratio = validity.astype(jnp.float32)[None, :, None] * numerator / denominator
    return jnp.transpose(ratio, (1, 0, 2)).reshape(col_count, span_len * span_len)

def reference(image, mask, flags):
    raw_volume = jnp.pad(image.astype(jnp.float32), ((0, 0), (BOX, BOX), (0, 0)))

    def norm_section(sec_index):
        raw_section = lax.dynamic_index_in_dim(raw_volume, sec_index.astype(jnp.int32), 0, False)
        tissue = lax.dynamic_index_in_dim(mask, sec_index.astype(jnp.int32), 0, False)
        return normalize(raw_section, tissue, BOX)
    masked = lax.map(norm_section, jnp.arange(SECTIONS, dtype=jnp.int32))
    following = jnp.concatenate([masked[1:], jnp.zeros_like(masked[:1])], axis=0)
    following = jnp.pad(following, ((0, 0), (SEARCH, SEARCH), (SEARCH, SEARCH)))

    def one_strip(strip_index):
        zero_index = jnp.zeros((), jnp.int32)
        sec_index = (strip_index // NPROW).astype(jnp.int32)
        row_index = (strip_index % NPROW).astype(jnp.int32)
        row_start = (row_index * PATCH).astype(jnp.int32)
        own_strip = lax.dynamic_slice(masked, (sec_index, row_start, zero_index), (1, PATCH, W))[0]
        extended = lax.dynamic_slice(following, (sec_index, row_start, zero_index), (1, PATCH + 2 * SEARCH, W + 2 * SEARCH))[0]
        validity = lax.dynamic_slice(flags, (sec_index, row_index, zero_index), (1, 1, PCOL))[0, 0]
        return strip_scores(own_strip, extended, validity)
    scores = lax.map(one_strip, jnp.arange(SECTIONS * NPROW, dtype=jnp.int32))
    return scores.reshape(SECTIONS, NPROW, PCOL, DISP)
```

```python
import jax
import jax.numpy as jnp
from jax import lax
from jax.experimental import pallas as pl
from jax.experimental.pallas import tpu as pltpu
from jax.sharding import PartitionSpec as P

PATCH = 128
SEARCH = 16
BOX = 8
SPAN = 2 * SEARCH + 1
SIDE = 2 * BOX + 1
PCOL = 4
W = PCOL * PATCH
EXT = PATCH + 2 * SEARCH
GROUP = 32
JN = PATCH // GROUP
FLOOR_SHARE = 0.25
EPSILON = 1e-05
F32 = jnp.float32
BF16 = jnp.bfloat16


def iota(shape, dim):
    return lax.broadcasted_iota(jnp.int32, shape, dim)


def mm(a, b):
    return jnp.dot(a, b, preferred_element_type=F32)


def band():
    r, c = iota((W, W // 2), 0), iota((W, W // 2), 1)
    return jnp.where(jnp.abs(r - PATCH - c) <= BOX, 1.0, 0.0).astype(BF16)


def across(x, g):
    lo = mm(x[:, : 3 * PATCH], g[PATCH:])
    hi = mm(x[:, PATCH:], g[: 3 * PATCH])
    return jnp.concatenate([lo, hi], axis=1)


def down(s, rows):
    n = rows + SIDE - 1
    s2 = s[: n - 1] + s[1:]
    s4 = s2[: n - 3] + s2[2:]
    s8 = s4[: n - 7] + s4[4:]
    s16 = s8[: n - 15] + s8[8:]
    return s16[:rows] + s[SIDE - 1 : SIDE - 1 + rows]


def normalized(x, tissue, g):
    rows = tissue.shape[0]
    xf = x.astype(F32)
    sq = xf * xf
    sq_hi = sq.astype(BF16)
    sq_lo = (sq - sq_hi.astype(F32)).astype(BF16)
    area = 1.0 / float(SIDE * SIDE)
    mean = down(across(x, g), rows) * area
    square = down(across(sq_hi, g) + across(sq_lo, g), rows) * area
    var = jnp.maximum(square - mean * mean, 0.0)
    scaled = (xf[BOX : BOX + rows] - mean) * lax.rsqrt(var + EPSILON)
    return (tissue * scaled).astype(BF16)


def correlate(a, b, flags_ref, out_ref, bpad, wgt, lhs, prod):
    r, c = iota((PATCH, PATCH), 0), iota((PATCH, PATCH), 1)
    flip = jnp.where((r // GROUP) * GROUP + (GROUP - 1 - r % GROUP) == c, 1.0, 0.0).astype(BF16)
    turned = [
        lax.dot_general(
            flip, a[:, PATCH * p : PATCH * (p + 1)], (((1,), (1,)), ((), ())), preferred_element_type=F32
        )
        for p in range(PCOL)
    ]
    bpad[...] = jnp.zeros_like(bpad)
    bpad[:, SEARCH : SEARCH + W] = b.astype(F32)
    wgt[...] = jnp.zeros_like(wgt)
    for j in range(JN):
        for p in range(PCOL):
            at = PATCH * p + GROUP * j
            wgt[pl.ds(j * PCOL * EXT + p * EXT, EXT), pl.ds(64 * p, 64)] = bpad[:, at : at + 64].astype(BF16)
    lane = iota((PATCH, PATCH), 1)
    tiles = PCOL * EXT // PATCH
    for u in range(SPAN):
        parts = [None] * (tiles + 1)
        for p in range(PCOL):
            t, o = divmod(EXT * p + u, PATCH)
            moved = pltpu.roll(turned[p], o, 1) if o else turned[p]
            for tile, keep in ((t, lane >= o), (t + 1, lane < o)):
                if tile == t + 1 and o == 0:
                    continue
                base = parts[tile]
                parts[tile] = jnp.where(keep, moved, 0.0 if base is None else base)
        for tile in range(tiles):
            val = parts[tile].astype(BF16)
            for j in range(JN):
                lhs[pl.ds(u * GROUP, GROUP), pl.ds((j * tiles + tile) * PATCH, PATCH)] = val[GROUP * j : GROUP * (j + 1)]
    prod[...] = mm(lhs[...], wgt[...])
    rows = []
    pieces = []
    for h in range(2):
        block = prod[:, pl.ds(PATCH * h, PATCH)].reshape(SPAN, JN, 8, PATCH)
        total = None
        for q in range(GROUP // 8):
            part = block[:, q].reshape(SPAN * 8, PATCH)
            part = part.reshape(SPAN, 8, PATCH)
            moved = pltpu.roll(part, PATCH - (GROUP - 1) + 8 * q, 2, stride=1, stride_axis=1)
            total = moved if total is None else total + moved
        pieces.append(jnp.sum(total, axis=1))
    numer = jnp.concatenate(pieces, axis=1)
    bf = b.astype(F32)
    sq = bf * bf
    sq_hi = sq.astype(BF16)
    sq_lo = (sq - sq_hi.astype(F32)).astype(BF16)
    ur, uc = iota((40, EXT), 0), iota((40, EXT), 1)
    vert = jnp.where((uc >= ur) & (uc < ur + PATCH), 1.0, 0.0).astype(BF16)
    col = mm(vert, sq_hi) + mm(vert, sq_lo)
    col_hi = col.astype(BF16)
    col_lo = (col - col_hi.astype(F32)).astype(BF16)
    xr, xc = iota((W, 64 * PCOL), 0), iota((W, 64 * PCOL), 1)
    start = (xc // 64) * PATCH + (xc % 64) - SEARCH
    horiz = jnp.where((xr >= start) & (xr < start + PATCH), 1.0, 0.0).astype(BF16)
    energy_next = (mm(col_hi, horiz) + mm(col_lo, horiz))[:SPAN]
    af = a.astype(F32)
    own = jnp.sum(af * af, axis=0, keepdims=True)
    own_hi = own.astype(BF16)
    own_lo = (own - own_hi.astype(F32)).astype(BF16)
    same = jnp.where(xr // PATCH == xc // 64, 1.0, 0.0).astype(BF16)
    own8 = jnp.concatenate([own_hi, own_lo, jnp.zeros((14, W), BF16)], axis=0)
    own_sum = mm(own8, same)
    energy_own = own_sum[0:1] + own_sum[1:2]
    floor_value = FLOOR_SHARE * PATCH * PATCH
    scale = lax.rsqrt(jnp.maximum(energy_own, floor_value)) * lax.rsqrt(jnp.maximum(energy_next, floor_value))
    score = numer * scale
    score = jnp.concatenate([score, jnp.zeros((40 - SPAN, 64 * PCOL), F32)], axis=0)
    ur, lane = iota((40, PATCH), 0), iota((40, PATCH), 1)
    for h in range(2):
        half = score[:, PATCH * h : PATCH * (h + 1)]
        for s in range(2):
            p = 2 * h + s
            flag = flags_ref[p].astype(F32)
            lines = []
            for k in range(5):
                rows8 = (half * flag)[8 * k : 8 * k + 8]
                base = (8 * k - 64 * s) % PATCH
                rows8 = pltpu.roll(rows8, base, 1) if base else rows8
                rows8 = pltpu.roll(rows8, 0, 1, stride=16, stride_axis=0)
                lines.append(pltpu.roll(rows8, 0, 1, stride=17, stride_axis=0))
            moved = jnp.concatenate(lines, axis=0)
            for t in range(9):
                at = t * PATCH + lane
                pick = (at >= SPAN * ur) & (at < SPAN * ur + SPAN)
                line = jnp.sum(jnp.where(pick, moved, 0.0), axis=0, keepdims=True)
                wide = min(PATCH, SPAN * SPAN - t * PATCH)
                out_ref[p : p + 1, t * PATCH : t * PATCH + wide] = line[:, :wide]


VMEM = pl.BlockSpec(memory_space=pltpu.VMEM)
SMEM = pl.BlockSpec(memory_space=pltpu.SMEM)
HALO = 32


def normalize_body(low_ref, mid_ref, high_ref, tissue_ref, out_ref):
    low, high = low_ref[...], high_ref[...]
    x = jnp.concatenate([low[SEARCH - BOX : HALO], mid_ref[...], high[: HALO - (SEARCH - BOX)]], axis=0)
    tissue = jnp.concatenate(
        [low[HALO:].astype(F32), tissue_ref[...].astype(F32), high[HALO:].astype(F32)], axis=0
    )
    out_ref[...] = normalized(x, tissue, band())


def correlate_body(own_ref, next_ref, flags_ref, out_ref, *scratch):
    correlate(own_ref[SEARCH : SEARCH + PATCH], next_ref[...], flags_ref, out_ref, *scratch)


def halo(image, tissue, top):
    if top:
        return jnp.concatenate([image[:HALO], tissue[:SEARCH].astype(BF16)], axis=0)
    return jnp.concatenate([image[-HALO:], tissue[-SEARCH:].astype(BF16)], axis=0)


def shards(image, mask, flags):
    image, mask, flags = image[0], mask[0], flags[0, 0]
    count = lax.axis_size("xy")
    forward = [(i, i + 1) for i in range(count - 1)]
    backward = [(b, a) for a, b in forward]
    low = lax.ppermute(halo(image, mask, False), "xy", forward)
    high = lax.ppermute(halo(image, mask, True), "xy", backward)
    own = pl.pallas_call(
        normalize_body,
        out_shape=jax.ShapeDtypeStruct((EXT, W), BF16),
        in_specs=[VMEM] * 4,
        out_specs=VMEM,
        compiler_params=pltpu.CompilerParams(vmem_limit_bytes=48 << 20),
    )(low, image, high, mask)
    sections = lax.axis_size("sec")
    following = lax.ppermute(own, "sec", [(s + 1, s) for s in range(sections - 1)])
    scores = pl.pallas_call(
        correlate_body,
        out_shape=jax.ShapeDtypeStruct((PCOL, SPAN * SPAN), F32),
        in_specs=[VMEM, VMEM, SMEM],
        out_specs=VMEM,
        scratch_shapes=[
            pltpu.VMEM((EXT, W + PATCH), F32),
            pltpu.VMEM((JN * PCOL * EXT, 64 * PCOL), BF16),
            pltpu.VMEM((SPAN * GROUP, JN * PCOL * EXT), BF16),
            pltpu.VMEM((SPAN * GROUP, 64 * PCOL), F32),
        ],
        compiler_params=pltpu.CompilerParams(vmem_limit_bytes=48 << 20),
    )(own, following, flags)
    return scores[None, None]


def solution(mesh):
    placed = (P("sec", "xy", None), P("sec", "xy", None), P("sec", "xy", None))
    return jax.shard_map(
        shards, mesh=mesh, in_specs=placed, out_specs=P("sec", "xy", None, None), check_vma=False
    )
```

```python
import jax
import jax.numpy as jnp
from jax import lax
from jax.experimental import pallas as pl
from jax.experimental.pallas import tpu as pltpu
from jax.sharding import PartitionSpec as P

PATCH = 128
SEARCH = 16
BOX = 8
SPAN = 2 * SEARCH + 1
SIDE = 2 * BOX + 1
PCOL = 4
W = PCOL * PATCH
EXT = PATCH + 2 * SEARCH
GROUP = 32
JN = PATCH // GROUP
FLOOR = 0.25 * PATCH * PATCH
EPSILON = 1e-05
F32 = jnp.float32
BF16 = jnp.bfloat16


def iota(shape, dim):
    return lax.broadcasted_iota(jnp.int32, shape, dim)


def mm(a, b):
    return jnp.dot(a, b, preferred_element_type=F32)


def band():
    r, c = iota((W, W // 2), 0), iota((W, W // 2), 1)
    return jnp.where(jnp.abs(r - PATCH - c) <= BOX, 1.0, 0.0).astype(BF16)


def across(x, g):
    lo = mm(x[:, : 3 * PATCH], g[PATCH:])
    hi = mm(x[:, PATCH:], g[: 3 * PATCH])
    return jnp.concatenate([lo, hi], axis=1)


def down(s, rows):
    n = rows + SIDE - 1
    s2 = s[: n - 1] + s[1:]
    s4 = s2[: n - 3] + s2[2:]
    s8 = s4[: n - 7] + s4[4:]
    s16 = s8[: n - 15] + s8[8:]
    return s16[:rows] + s[SIDE - 1 : SIDE - 1 + rows]


def normalized(x, tissue, g):
    rows = tissue.shape[0]
    xf = x
    x = xf.astype(BF16)
    sq = xf * xf
    sq_hi = sq.astype(BF16)
    sq_lo = (sq - sq_hi.astype(F32)).astype(BF16)
    area = 1.0 / float(SIDE * SIDE)
    mean = down(across(x, g), rows) * area
    square = down(across(sq_hi, g) + across(sq_lo, g), rows) * area
    var = jnp.maximum(square - mean * mean, 0.0)
    scaled = (xf[BOX : BOX + rows] - mean) * lax.rsqrt(var + EPSILON)
    return (tissue * scaled).astype(BF16)


def shifted(a, lhs, own_scale):
    r, c = iota((PATCH, PATCH), 0), iota((PATCH, PATCH), 1)
    flip = jnp.where((r // GROUP) * GROUP + (GROUP - 1 - r % GROUP) == c, 1.0, 0.0).astype(BF16)
    turned = [
        lax.dot_general(
            flip, a[:, PATCH * p : PATCH * (p + 1)], (((1,), (1,)), ((), ())), preferred_element_type=F32
        )
        for p in range(PCOL)
    ]
    lane = iota((PATCH, PATCH), 1)
    tiles = PCOL * EXT // PATCH
    for u in range(SPAN):
        parts = [None] * (tiles + 1)
        for p in range(PCOL):
            t, o = divmod(EXT * p + u, PATCH)
            moved = pltpu.roll(turned[p], o, 1) if o else turned[p]
            for tile, keep in ((t, lane >= o), (t + 1, lane < o)):
                if tile == t + 1 and o == 0:
                    continue
                base = parts[tile]
                parts[tile] = jnp.where(keep, moved, 0.0 if base is None else base)
        for tile in range(tiles):
            val = parts[tile].astype(BF16)
            for j in range(JN):
                lhs[pl.ds(u * GROUP, GROUP), pl.ds((j * tiles + tile) * PATCH, PATCH)] = val[GROUP * j : GROUP * (j + 1)]
    xr, xc = iota((W, 64 * PCOL), 0), iota((W, 64 * PCOL), 1)
    af = a.astype(F32)
    own = jnp.sum(af * af, axis=0, keepdims=True)
    own_hi = own.astype(BF16)
    own_lo = (own - own_hi.astype(F32)).astype(BF16)
    same = jnp.where(xr // PATCH == xc // 64, 1.0, 0.0).astype(BF16)
    own8 = jnp.concatenate([own_hi, own_lo, jnp.zeros((14, W), BF16)], axis=0)
    own_sum = mm(own8, same)
    energy_own = own_sum[0:1] + own_sum[1:2]
    own_scale[...] = jnp.broadcast_to(lax.rsqrt(jnp.maximum(energy_own, FLOOR)), own_scale.shape)


def correlate(b, own_scale, flags_ref, out_ref, lhs, bpad, wgt, prod):
    bpad[...] = jnp.zeros_like(bpad)
    bpad[:, SEARCH : SEARCH + W] = b.astype(F32)
    wgt[...] = jnp.zeros_like(wgt)
    for j in range(JN):
        for p in range(PCOL):
            at = PATCH * p + GROUP * j
            wgt[pl.ds(j * PCOL * EXT + p * EXT, EXT), pl.ds(64 * p, 64)] = bpad[:, at : at + 64].astype(BF16)
    prod[...] = mm(lhs[...], wgt[...])
    rows = []
    pieces = []
    for h in range(2):
        block = prod[:, pl.ds(PATCH * h, PATCH)].reshape(SPAN, JN, 8, PATCH)
        total = None
        for q in range(GROUP // 8):
            part = block[:, q].reshape(SPAN * 8, PATCH)
            part = part.reshape(SPAN, 8, PATCH)
            moved = pltpu.roll(part, PATCH - (GROUP - 1) + 8 * q, 2, stride=1, stride_axis=1)
            total = moved if total is None else total + moved
        pieces.append(jnp.sum(total, axis=1))
    numer = jnp.concatenate(pieces, axis=1)
    bf = b.astype(F32)
    sq = bf * bf
    sq_hi = sq.astype(BF16)
    sq_lo = (sq - sq_hi.astype(F32)).astype(BF16)
    ur, uc = iota((40, EXT), 0), iota((40, EXT), 1)
    vert = jnp.where((uc >= ur) & (uc < ur + PATCH), 1.0, 0.0).astype(BF16)
    col = mm(vert, sq_hi) + mm(vert, sq_lo)
    col_hi = col.astype(BF16)
    col_lo = (col - col_hi.astype(F32)).astype(BF16)
    xr, xc = iota((W, 64 * PCOL), 0), iota((W, 64 * PCOL), 1)
    start = (xc // 64) * PATCH + (xc % 64) - SEARCH
    horiz = jnp.where((xr >= start) & (xr < start + PATCH), 1.0, 0.0).astype(BF16)
    energy_next = (mm(col_hi, horiz) + mm(col_lo, horiz))[:SPAN]
    scale = own_scale[0:1] * lax.rsqrt(jnp.maximum(energy_next, FLOOR))
    score = numer * scale
    score = jnp.concatenate([score, jnp.zeros((40 - SPAN, 64 * PCOL), F32)], axis=0)
    ur, lane = iota((40, PATCH), 0), iota((40, PATCH), 1)
    for h in range(2):
        half = score[:, PATCH * h : PATCH * (h + 1)]
        for s in range(2):
            p = 2 * h + s
            flag = flags_ref[p].astype(F32)
            lines = []
            for k in range(5):
                rows8 = (half * flag)[8 * k : 8 * k + 8]
                base = (8 * k - 64 * s) % PATCH
                rows8 = pltpu.roll(rows8, base, 1) if base else rows8
                rows8 = pltpu.roll(rows8, 0, 1, stride=16, stride_axis=0)
                lines.append(pltpu.roll(rows8, 0, 1, stride=17, stride_axis=0))
            moved = jnp.concatenate(lines, axis=0)
            for t in range(9):
                at = t * PATCH + lane
                pick = (at >= SPAN * ur) & (at < SPAN * ur + SPAN)
                line = jnp.sum(jnp.where(pick, moved, 0.0), axis=0, keepdims=True)
                wide = min(PATCH, SPAN * SPAN - t * PATCH)
                out_ref[p : p + 1, t * PATCH : t * PATCH + wide] = line[:, :wide]


VMEM = pl.BlockSpec(memory_space=pltpu.VMEM)
SMEM = pl.BlockSpec(memory_space=pltpu.SMEM)
RIM = 2 * BOX
INNER = PATCH - 2 * BOX
SLAB = RIM + 2 * BOX
FAR_SLAB = 40
FAR = 7
PARAMS = pltpu.CompilerParams(vmem_limit_bytes=48 << 20)
LONG = pl.CostEstimate(flops=1 << 33, bytes_accessed=1 << 20, transcendentals=0)
SHORT = pl.CostEstimate(flops=1, bytes_accessed=1, transcendentals=0)


def prepare_body(image_hbm, tissue_hbm, core_ref, first_ref, second_ref, first_far_ref, second_far_ref, image, tissue, sems):
    copies = [
        pltpu.make_async_copy(image_hbm, image, sems.at[0]),
        pltpu.make_async_copy(tissue_hbm, tissue, sems.at[1]),
    ]
    for copy in copies:
        copy.start()
    for copy in copies:
        copy.wait()
    x = image[...].astype(F32)
    marks = tissue[...].astype(F32)
    inner = normalized(x, marks[BOX : PATCH - BOX], band())
    top, bottom = x[:RIM], x[PATCH - RIM :]
    top_marks, bottom_marks = marks[:BOX], marks[PATCH - BOX :]
    core_ref[:INNER] = inner
    core_ref[INNER:] = jnp.concatenate([top, bottom, top_marks, bottom_marks], axis=0).astype(BF16)
    inner = inner.astype(F32)
    upper = jnp.concatenate([inner[:BOX], top, top_marks], axis=0).astype(BF16)
    lower = jnp.concatenate([inner[INNER - BOX :], bottom, bottom_marks], axis=0).astype(BF16)
    even = lax.axis_index("xy") % 2 == 0

    @pl.when(even)
    def _():
        first_ref[...] = upper
        second_ref[...] = lower
        first_far_ref[:SLAB] = upper
        second_far_ref[:SLAB] = lower

    @pl.when(jnp.logical_not(even))
    def _():
        first_ref[...] = lower
        second_ref[...] = upper
        first_far_ref[:SLAB] = lower
        second_far_ref[:SLAB] = upper


def completed(core, first, second):
    keep = jnp.where(lax.axis_index("xy") % 2 == 0, 1.0, 0.0).astype(F32)
    core, first, second = core.astype(F32), first.astype(F32), second.astype(F32)
    low = first * keep + second * (1.0 - keep)
    high = second * keep + first * (1.0 - keep)
    edges = core[INNER:]
    g = band()
    x = jnp.concatenate([low[BOX : BOX + RIM], edges[:RIM]], axis=0)
    tissue = jnp.concatenate([low[BOX + RIM :], edges[2 * RIM : 2 * RIM + BOX]], axis=0)
    above = normalized(x, tissue, g).astype(F32)
    x = jnp.concatenate([edges[RIM : 2 * RIM], high[BOX : BOX + RIM]], axis=0)
    tissue = jnp.concatenate([edges[2 * RIM + BOX :], high[BOX + RIM :]], axis=0)
    below = normalized(x, tissue, g).astype(F32)
    return jnp.concatenate([low[:BOX], above, core[:INNER], below, high[:BOX]], axis=0)


def complete_body(core_ref, first_ref, second_ref, out_ref):
    out_ref[...] = completed(core_ref[...], first_ref[...], second_ref[...]).astype(BF16)


def shifted_body(own_ref, lhs_ref, own_scale_ref):
    shifted(own_ref[SEARCH : SEARCH + PATCH], lhs_ref, own_scale_ref)


def is_far():
    return lax.axis_index("sec") == FAR


def far_body(core_ref, first_ref, second_ref, own_scale_ref, out_ref):
    @pl.when(is_far())
    def _():
        out_ref[...] = completed(core_ref[...], first_ref[:SLAB], second_ref[:SLAB]).astype(BF16)


def correlate_body(next_ref, far_ref, lhs_ref, own_scale_ref, flags_ref, out_ref, *scratch):
    b = jnp.where(is_far(), far_ref[...].astype(F32), next_ref[...].astype(F32)).astype(BF16)
    correlate(b, own_scale_ref[...], flags_ref, out_ref, lhs_ref, *scratch)


def odd_partner(i):
    return i - 1 if i % 2 == 0 else i + 1


def even_partner(i):
    return i + 1 if i % 2 == 0 else i - 1


def call(body, out_shape, operands, in_specs=None, scratch=(), cost=None):
    several = isinstance(out_shape, tuple)
    return pl.pallas_call(
        body,
        out_shape=out_shape,
        in_specs=in_specs or [VMEM] * len(operands),
        out_specs=(VMEM,) * len(out_shape) if several else VMEM,
        scratch_shapes=scratch,
        compiler_params=PARAMS,
        cost_estimate=cost,
    )(*operands)


def shards(image, mask, flags):
    image, mask, flags = image[0], mask[0], flags[0, 0]
    strips, sections = lax.axis_size("xy"), lax.axis_size("sec")
    odd = [(i, odd_partner(i)) for i in range(strips) if 0 <= odd_partner(i) < strips]
    even = [(i, even_partner(i)) for i in range(strips)]

    def rows(count):
        return jax.ShapeDtypeStruct((count, W), BF16)

    core, first, second, first_far, second_far = call(
        prepare_body,
        (rows(PATCH + 2 * RIM), rows(SLAB), rows(SLAB), rows(FAR_SLAB), rows(FAR_SLAB)),
        (image, mask),
        in_specs=[pl.BlockSpec(memory_space=pl.ANY)] * 2,
        scratch=[
            pltpu.VMEM((PATCH, W), BF16),
            pltpu.VMEM((PATCH, W), jnp.int32),
            pltpu.SemaphoreType.DMA((2,)),
        ],
    )

    def from_far(block, pairs):
        route = [((FAR + 1) * strips + a, FAR * strips + b) for a, b in pairs]
        return lax.ppermute(block, ("sec", "xy"), route)

    core_far = from_far(core, [(i, i) for i in range(strips)])
    first_far = from_far(first_far, odd)
    second_far = from_far(second_far, even)
    first = lax.ppermute(first, "xy", odd)
    second = lax.ppermute(second, "xy", even)
    own = call(complete_body, rows(EXT), (core, first, second), cost=SHORT)
    following = lax.ppermute(own, "sec", [(s + 1, s) for s in range(sections - 1) if s != FAR])
    lhs, own_scale = call(
        shifted_body,
        (
            jax.ShapeDtypeStruct((SPAN * GROUP, JN * PCOL * EXT), BF16),
            jax.ShapeDtypeStruct((8, 64 * PCOL), F32),
        ),
        (own,),
        cost=SHORT,
    )
    far = call(far_body, rows(EXT), (core_far, first_far, second_far, own_scale), cost=LONG)
    scores = call(
        correlate_body,
        jax.ShapeDtypeStruct((PCOL, SPAN * SPAN), F32),
        (following, far, lhs, own_scale, flags),
        in_specs=[VMEM] * 4 + [SMEM],
        scratch=[
            pltpu.VMEM((EXT, W + PATCH), F32),
            pltpu.VMEM((JN * PCOL * EXT, 64 * PCOL), BF16),
            pltpu.VMEM((SPAN * GROUP, 64 * PCOL), F32),
        ],
    )
    return scores[None, None]


def solution(mesh):
    placed = (P("sec", "xy", None), P("sec", "xy", None), P("sec", "xy", None))
    return jax.shard_map(
        shards, mesh=mesh, in_specs=placed, out_specs=P("sec", "xy", None, None), check_vma=False
    )
```

```python
import jax
import jax.numpy as jnp
from jax import lax
from jax.experimental import pallas as pl
from jax.experimental.pallas import tpu as pltpu
from jax.sharding import PartitionSpec as P

PATCH = 128
SEARCH = 16
BOX = 8
SPAN = 2 * SEARCH + 1
SIDE = 2 * BOX + 1
PCOL = 4
W = PCOL * PATCH
EXT = PATCH + 2 * SEARCH
GROUP = 32
JN = PATCH // GROUP
FLOOR = 0.25 * PATCH * PATCH
EPSILON = 1e-05
F32 = jnp.float32
BF16 = jnp.bfloat16


def iota(shape, dim):
    return lax.broadcasted_iota(jnp.int32, shape, dim)


def mm(a, b):
    return jnp.dot(a, b, preferred_element_type=F32)


def band():
    r, c = iota((W, W // 2), 0), iota((W, W // 2), 1)
    return jnp.where(jnp.abs(r - PATCH - c) <= BOX, 1.0, 0.0).astype(BF16)


def across(x, g):
    lo = mm(x[:, : 3 * PATCH], g[PATCH:])
    hi = mm(x[:, PATCH:], g[: 3 * PATCH])
    return jnp.concatenate([lo, hi], axis=1)


def down(s, rows):
    n = rows + SIDE - 1
    s2 = s[: n - 1] + s[1:]
    s4 = s2[: n - 3] + s2[2:]
    s8 = s4[: n - 7] + s4[4:]
    s16 = s8[: n - 15] + s8[8:]
    return s16[:rows] + s[SIDE - 1 : SIDE - 1 + rows]


def normalized(x, tissue, g):
    rows = tissue.shape[0]
    xf = x
    x = xf.astype(BF16)
    sq = xf * xf
    sq_hi = sq.astype(BF16)
    sq_lo = (sq - sq_hi.astype(F32)).astype(BF16)
    area = 1.0 / float(SIDE * SIDE)
    mean = down(across(x, g), rows) * area
    square = down(across(sq_hi, g) + across(sq_lo, g), rows) * area
    var = jnp.maximum(square - mean * mean, 0.0)
    scaled = (xf[BOX : BOX + rows] - mean) * lax.rsqrt(var + EPSILON)
    return (tissue * scaled).astype(BF16)


def shifted(a, valid, lhs, own_scale):
    r, c = iota((PATCH, PATCH), 0), iota((PATCH, PATCH), 1)
    flip = jnp.where((r // GROUP) * GROUP + (GROUP - 1 - r % GROUP) == c, 1.0, 0.0).astype(BF16)
    turned = [
        lax.dot_general(
            flip, a[:, PATCH * p : PATCH * (p + 1)], (((1,), (1,)), ((), ())), preferred_element_type=F32
        )
        for p in range(PCOL)
    ]
    lane = iota((PATCH, PATCH), 1)
    tiles = PCOL * EXT // PATCH
    for u in range(SPAN):
        parts = [None] * (tiles + 1)
        for p in range(PCOL):
            t, o = divmod(EXT * p + u, PATCH)
            moved = pltpu.roll(turned[p], o, 1) if o else turned[p]
            for tile, keep in ((t, lane >= o), (t + 1, lane < o)):
                if tile == t + 1 and o == 0:
                    continue
                base = parts[tile]
                parts[tile] = jnp.where(keep, moved, 0.0 if base is None else base)
        for tile in range(tiles):
            val = parts[tile].astype(BF16)
            for j in range(JN):
                lhs[pl.ds(u * GROUP, GROUP), pl.ds((j * tiles + tile) * PATCH, PATCH)] = val[GROUP * j : GROUP * (j + 1)]
    xr, xc = iota((W, 64 * PCOL), 0), iota((W, 64 * PCOL), 1)
    af = a.astype(F32)
    own = jnp.sum(af * af, axis=0, keepdims=True)
    own_hi = own.astype(BF16)
    own_lo = (own - own_hi.astype(F32)).astype(BF16)
    same = jnp.where(xr // PATCH == xc // 64, 1.0, 0.0).astype(BF16)
    own8 = jnp.concatenate([own_hi, own_lo, jnp.zeros((14, W), BF16)], axis=0)
    own_sum = mm(own8, same)
    energy_own = own_sum[0:1] + own_sum[1:2]
    own_scale[...] = valid * lax.rsqrt(jnp.maximum(energy_own, FLOOR))


def correlate(b, own_scale, out_ref, lhs, wide, wgt, prod):
    wide[:, :PATCH] = jnp.zeros((EXT, PATCH), F32)
    wide[:, W:] = jnp.zeros((EXT, PATCH), F32)
    wide[:, SEARCH : SEARCH + W] = b
    lane = iota((EXT, PATCH), 1)
    for p in range(PCOL):
        h, q = divmod(p, 2)
        one, two = wide[:, PATCH * p : PATCH * (p + 1)], wide[:, PATCH * (p + 1) : PATCH * (p + 2)]
        for j in range(JN):
            turn = (64 * q - GROUP * j) % PATCH
            piece = pltpu.roll(one, turn, 1) if turn else one
            if j == JN - 1:
                piece = jnp.where(lane < 64 * q + GROUP, piece, pltpu.roll(two, turn, 1) if turn else two)
            rows = pl.ds((j * PCOL + p) * EXT, EXT)
            keep = lane < 64 if q == 0 else lane >= 64
            wgt[rows, pl.ds(PATCH * h, PATCH)] = jnp.where(keep, piece, 0.0).astype(BF16)
            wgt[rows, pl.ds(PATCH * (1 - h), PATCH)] = jnp.zeros((EXT, PATCH), BF16)
    prod[...] = mm(lhs[...], wgt[...])
    sq = wide[...] * wide[...]
    sq_hi = sq.astype(BF16)
    sq_lo = (sq - sq_hi.astype(F32)).astype(BF16)
    r, c = iota((40, EXT), 0), iota((40, EXT), 1)
    vert = jnp.where((c >= r) & (c < r + PATCH), 1.0, 0.0).astype(BF16)
    col = mm(vert, sq_hi) + mm(vert, sq_lo)
    col_hi = col.astype(BF16)
    col_lo = (col - col_hi.astype(F32)).astype(BF16)
    parts = jnp.concatenate([col_hi, col_lo], axis=0)
    r, c = iota((2 * PATCH, PATCH), 0), iota((2 * PATCH, PATCH), 1) % 64
    horiz = jnp.where((r >= c) & (r < c + PATCH), 1.0, 0.0).astype(BF16)
    sums = [mm(parts[:, PATCH * p : PATCH * (p + 2)], horiz) for p in range(PCOL)]
    left = iota((40, PATCH), 1) < 64
    energies = [jnp.where(left, sums[2 * h][:40] + sums[2 * h][40:], sums[2 * h + 1][:40] + sums[2 * h + 1][40:]) for h in range(2)]
    ur, lane = iota((40, PATCH), 0), iota((40, PATCH), 1)
    for h in range(2):
        block = prod[:, pl.ds(PATCH * h, PATCH)].reshape(SPAN, JN, 8, PATCH)
        total = None
        for q in range(GROUP // 8):
            part = block[:, q]
            moved = pltpu.roll(part, PATCH - (GROUP - 1) + 8 * q, 2, stride=1, stride_axis=1)
            total = moved if total is None else total + moved
        numer = jnp.sum(total, axis=1)
        numer = jnp.concatenate([numer, jnp.zeros((40 - SPAN, PATCH), F32)], axis=0)
        scale = own_scale[0:1, PATCH * h : PATCH * (h + 1)] * lax.rsqrt(jnp.maximum(energies[h], FLOOR))
        score = numer * scale
        lines = []
        for k in range(5):
            line = score[8 * k : 8 * k + 8]
            line = pltpu.roll(line, 8 * k, 1) if k else line
            line = pltpu.roll(line, 0, 1, stride=16, stride_axis=0)
            lines.append(pltpu.roll(line, 0, 1, stride=17, stride_axis=0))
        both = jnp.concatenate(lines, axis=0)
        for q, moved in enumerate((both, pltpu.roll(both, 64, 1))):
            p = 2 * h + q
            for t in range(9):
                at = t * PATCH + lane
                pick = (at >= SPAN * ur) & (at < SPAN * ur + SPAN)
                line = jnp.sum(jnp.where(pick, moved, 0.0), axis=0, keepdims=True)
                count = min(PATCH, SPAN * SPAN - t * PATCH)
                out_ref[p : p + 1, t * PATCH : t * PATCH + count] = line[:, :count]


VMEM = pl.BlockSpec(memory_space=pltpu.VMEM)
RIM = 2 * BOX
INNER = PATCH - 2 * BOX
SLAB = RIM + 2 * BOX
FAR_SLAB = 40
FAR = 7
PARAMS = pltpu.CompilerParams(vmem_limit_bytes=48 << 20)
LONG = pl.CostEstimate(flops=1 << 33, bytes_accessed=1 << 20, transcendentals=0)
SHORT = pl.CostEstimate(flops=1, bytes_accessed=1, transcendentals=0)


def prepare_body(
    image_hbm, tissue_hbm, flags_hbm, core_ref, first_ref, second_ref, first_far_ref, second_far_ref, valid_ref,
    image, tissue, flags, sems,
):
    copies = [
        pltpu.make_async_copy(image_hbm, image, sems.at[0]),
        pltpu.make_async_copy(tissue_hbm, tissue, sems.at[1]),
        pltpu.make_async_copy(flags_hbm, flags, sems.at[2]),
    ]
    for copy in copies:
        copy.start()
    for copy in copies:
        copy.wait()
    x = image[...].astype(F32)
    marks = tissue[...].astype(F32)
    inner = normalized(x, marks[BOX : PATCH - BOX], band())
    top, bottom = x[:RIM], x[PATCH - RIM :]
    top_marks, bottom_marks = marks[:BOX], marks[PATCH - BOX :]
    core_ref[:INNER] = inner
    core_ref[INNER:] = jnp.concatenate([top, bottom, top_marks, bottom_marks], axis=0).astype(BF16)
    inner = inner.astype(F32)
    upper = jnp.concatenate([inner[:BOX], top, top_marks], axis=0).astype(BF16)
    lower = jnp.concatenate([inner[INNER - BOX :], bottom, bottom_marks], axis=0).astype(BF16)
    patch = iota((8, 64 * PCOL), 1) // 64
    valid = jnp.zeros((8, 64 * PCOL), jnp.int32)
    for p in range(PCOL):
        valid = jnp.where(patch == p, flags[p], valid)
    valid_ref[...] = valid.astype(F32)
    even = lax.axis_index("xy") % 2 == 0

    @pl.when(even)
    def _():
        first_ref[...] = upper
        second_ref[...] = lower
        first_far_ref[:SLAB] = upper
        second_far_ref[:SLAB] = lower

    @pl.when(jnp.logical_not(even))
    def _():
        first_ref[...] = lower
        second_ref[...] = upper
        first_far_ref[:SLAB] = lower
        second_far_ref[:SLAB] = upper


def completed(core, first, second):
    keep = jnp.where(lax.axis_index("xy") % 2 == 0, 1.0, 0.0).astype(F32)
    core, first, second = core.astype(F32), first.astype(F32), second.astype(F32)
    low = first * keep + second * (1.0 - keep)
    high = second * keep + first * (1.0 - keep)
    edges = core[INNER:]
    g = band()
    x = jnp.concatenate([low[BOX : BOX + RIM], edges[:RIM]], axis=0)
    tissue = jnp.concatenate([low[BOX + RIM :], edges[2 * RIM : 2 * RIM + BOX]], axis=0)
    above = normalized(x, tissue, g).astype(F32)
    x = jnp.concatenate([edges[RIM : 2 * RIM], high[BOX : BOX + RIM]], axis=0)
    tissue = jnp.concatenate([edges[2 * RIM + BOX :], high[BOX + RIM :]], axis=0)
    below = normalized(x, tissue, g).astype(F32)
    return jnp.concatenate([low[:BOX], above, core[:INNER], below, high[:BOX]], axis=0)


def complete_body(core_ref, first_ref, second_ref, out_ref):
    out_ref[...] = completed(core_ref[...], first_ref[...], second_ref[...]).astype(BF16)


def shifted_body(own_ref, valid_ref, lhs_ref, own_scale_ref):
    shifted(own_ref[SEARCH : SEARCH + PATCH], valid_ref[...], lhs_ref, own_scale_ref)


def is_far():
    return lax.axis_index("sec") == FAR


def far_body(core_ref, first_ref, second_ref, own_scale_ref, out_ref):
    @pl.when(is_far())
    def _():
        out_ref[...] = completed(core_ref[...], first_ref[:SLAB], second_ref[:SLAB]).astype(BF16)


def correlate_body(next_ref, far_ref, lhs_ref, own_scale_ref, out_ref, *scratch):
    b = jnp.where(is_far(), far_ref[...].astype(F32), next_ref[...].astype(F32))
    correlate(b, own_scale_ref[...], out_ref, lhs_ref, *scratch)


def odd_partner(i):
    return i - 1 if i % 2 == 0 else i + 1


def even_partner(i):
    return i + 1 if i % 2 == 0 else i - 1


def call(body, out_shape, operands, in_specs=None, scratch=(), cost=None):
    several = isinstance(out_shape, tuple)
    return pl.pallas_call(
        body,
        out_shape=out_shape,
        in_specs=in_specs or [VMEM] * len(operands),
        out_specs=(VMEM,) * len(out_shape) if several else VMEM,
        scratch_shapes=scratch,
        compiler_params=PARAMS,
        cost_estimate=cost,
    )(*operands)


def shards(image, mask, flags):
    image, mask, flags = image[0], mask[0], flags[0, 0]
    strips, sections = lax.axis_size("xy"), lax.axis_size("sec")
    odd = [(i, odd_partner(i)) for i in range(strips) if 0 <= odd_partner(i) < strips]
    even = [(i, even_partner(i)) for i in range(strips)]

    def rows(count):
        return jax.ShapeDtypeStruct((count, W), BF16)

    core, first, second, first_far, second_far, valid = call(
        prepare_body,
        (rows(PATCH + 2 * RIM), rows(SLAB), rows(SLAB), rows(FAR_SLAB), rows(FAR_SLAB), jax.ShapeDtypeStruct((8, 64 * PCOL), F32)),
        tuple(pltpu.with_memory_space_constraint(x, pltpu.HBM) for x in (image, mask, flags)),
        in_specs=[pl.BlockSpec(memory_space=pltpu.HBM)] * 3,
        scratch=[
            pltpu.VMEM((PATCH, W), BF16),
            pltpu.VMEM((PATCH, W), jnp.int32),
            pltpu.SMEM((PCOL,), jnp.int32),
            pltpu.SemaphoreType.DMA((3,)),
        ],
    )

    def from_far(block, pairs):
        route = [((FAR + 1) * strips + a, FAR * strips + b) for a, b in pairs]
        return lax.ppermute(block, ("sec", "xy"), route)

    core_far = from_far(core, [(i, i) for i in range(strips)])
    first_far = from_far(first_far, odd)
    second_far = from_far(second_far, even)
    first = lax.ppermute(first, "xy", odd)
    second = lax.ppermute(second, "xy", even)
    own = call(complete_body, rows(EXT), (core, first, second), cost=SHORT)
    following = lax.ppermute(own, "sec", [(s + 1, s) for s in range(sections - 1) if s != FAR])
    lhs, own_scale = call(
        shifted_body,
        (
            jax.ShapeDtypeStruct((SPAN * GROUP, JN * PCOL * EXT), BF16),
            jax.ShapeDtypeStruct((8, 64 * PCOL), F32),
        ),
        (own, valid),
        cost=SHORT,
    )
    far = call(far_body, rows(EXT), (core_far, first_far, second_far, own_scale), cost=LONG)
    scores = call(
        correlate_body,
        jax.ShapeDtypeStruct((PCOL, SPAN * SPAN), F32),
        (following, far, lhs, own_scale),
        scratch=[
            pltpu.VMEM((EXT, W + PATCH), F32),
            pltpu.VMEM((JN * PCOL * EXT, 64 * PCOL), BF16),
            pltpu.VMEM((SPAN * GROUP, 64 * PCOL), F32),
        ],
    )
    return scores[None, None]


def solution(mesh):
    placed = (P("sec", "xy", None), P("sec", "xy", None), P("sec", "xy", None))
    return jax.shard_map(
        shards, mesh=mesh, in_specs=placed, out_specs=P("sec", "xy", None, None), check_vma=False
    )
```

```python
import jax
import jax.numpy as jnp
from jax import lax
from jax.experimental import pallas as pl
from jax.experimental.pallas import tpu as pltpu
from jax.sharding import PartitionSpec as P

PATCH = 128
SEARCH = 16
BOX = 8
SPAN = 2 * SEARCH + 1
SIDE = 2 * BOX + 1
PCOL = 4
W = PCOL * PATCH
EXT = PATCH + 2 * SEARCH
GROUP = 32
JN = PATCH // GROUP
FLOOR = 0.25 * PATCH * PATCH
EPSILON = 1e-05
F32 = jnp.float32
BF16 = jnp.bfloat16


def iota(shape, dim):
    return lax.broadcasted_iota(jnp.int32, shape, dim)


def mm(a, b):
    return jnp.dot(a, b, preferred_element_type=F32)


def band():
    r, c = iota((W, W // 2), 0), iota((W, W // 2), 1)
    return jnp.where(jnp.abs(r - PATCH - c) <= BOX, 1.0, 0.0).astype(BF16)


def across(x, g):
    lo = mm(x[:, : 3 * PATCH], g[PATCH:])
    hi = mm(x[:, PATCH:], g[: 3 * PATCH])
    return jnp.concatenate([lo, hi], axis=1)


def down(s, rows):
    n = rows + SIDE - 1
    s2 = s[: n - 1] + s[1:]
    s4 = s2[: n - 3] + s2[2:]
    s8 = s4[: n - 7] + s4[4:]
    s16 = s8[: n - 15] + s8[8:]
    return s16[:rows] + s[SIDE - 1 : SIDE - 1 + rows]


def standardized(x, rows, g):
    sq = x * x
    sq_hi = sq.astype(BF16)
    sq_lo = (sq - sq_hi.astype(F32)).astype(BF16)
    area = 1.0 / float(SIDE * SIDE)
    mean = down(across(x.astype(BF16), g), rows) * area
    square = down(across(sq_hi, g) + across(sq_lo, g), rows) * area
    var = jnp.maximum(square - mean * mean, 0.0)
    return (x[BOX : BOX + rows] - mean) * lax.rsqrt(var + EPSILON)


def normalized(x, tissue, g):
    return (tissue * standardized(x, tissue.shape[0], g)).astype(BF16)


def shifted(a, valid, lhs, own_scale):
    r, c = iota((PATCH, PATCH), 0), iota((PATCH, PATCH), 1)
    flip = jnp.where((r // GROUP) * GROUP + (GROUP - 1 - r % GROUP) == c, 1.0, 0.0).astype(BF16)
    turned = [
        lax.dot_general(
            flip, a[:, PATCH * p : PATCH * (p + 1)], (((1,), (1,)), ((), ())), preferred_element_type=F32
        )
        for p in range(PCOL)
    ]
    lane = iota((PATCH, PATCH), 1)
    tiles = PCOL * EXT // PATCH
    for u in range(SPAN):
        parts = [None] * (tiles + 1)
        for p in range(PCOL):
            t, o = divmod(EXT * p + u, PATCH)
            moved = pltpu.roll(turned[p], o, 1) if o else turned[p]
            for tile, keep in ((t, lane >= o), (t + 1, lane < o)):
                if tile == t + 1 and o == 0:
                    continue
                base = parts[tile]
                parts[tile] = jnp.where(keep, moved, 0.0 if base is None else base)
        for tile in range(tiles):
            val = parts[tile].astype(BF16)
            for j in range(JN):
                lhs[pl.ds(u * GROUP, GROUP), pl.ds((j * tiles + tile) * PATCH, PATCH)] = val[GROUP * j : GROUP * (j + 1)]
    xr, xc = iota((W, 64 * PCOL), 0), iota((W, 64 * PCOL), 1)
    af = a.astype(F32)
    own = jnp.sum(af * af, axis=0, keepdims=True)
    own_hi = own.astype(BF16)
    own_lo = (own - own_hi.astype(F32)).astype(BF16)
    same = jnp.where(xr // PATCH == xc // 64, 1.0, 0.0).astype(BF16)
    own8 = jnp.concatenate([own_hi, own_lo, jnp.zeros((14, W), BF16)], axis=0)
    own_sum = mm(own8, same)
    energy_own = own_sum[0:1] + own_sum[1:2]
    own_scale[...] = valid * lax.rsqrt(jnp.maximum(energy_own, FLOOR))


def correlate(b, own_scale, out_ref, lhs, wide, wgt, prod):
    wide[:, :PATCH] = jnp.zeros((EXT, PATCH), F32)
    wide[:, W:] = jnp.zeros((EXT, PATCH), F32)
    wide[:, SEARCH : SEARCH + W] = b
    lane = iota((EXT, PATCH), 1)
    for p in range(PCOL):
        h, q = divmod(p, 2)
        one, two = wide[:, PATCH * p : PATCH * (p + 1)], wide[:, PATCH * (p + 1) : PATCH * (p + 2)]
        for j in range(JN):
            turn = (64 * q - GROUP * j) % PATCH
            piece = pltpu.roll(one, turn, 1) if turn else one
            if j == JN - 1:
                piece = jnp.where(lane < 64 * q + GROUP, piece, pltpu.roll(two, turn, 1) if turn else two)
            rows = pl.ds((j * PCOL + p) * EXT, EXT)
            keep = lane < 64 if q == 0 else lane >= 64
            wgt[rows, pl.ds(PATCH * h, PATCH)] = jnp.where(keep, piece, 0.0).astype(BF16)
            wgt[rows, pl.ds(PATCH * (1 - h), PATCH)] = jnp.zeros((EXT, PATCH), BF16)
    prod[...] = mm(lhs[...], wgt[...])
    sq = wide[...] * wide[...]
    sq_hi = sq.astype(BF16)
    sq_lo = (sq - sq_hi.astype(F32)).astype(BF16)
    r, c = iota((40, EXT), 0), iota((40, EXT), 1)
    vert = jnp.where((c >= r) & (c < r + PATCH), 1.0, 0.0).astype(BF16)
    col = mm(vert, sq_hi) + mm(vert, sq_lo)
    col_hi = col.astype(BF16)
    col_lo = (col - col_hi.astype(F32)).astype(BF16)
    parts = jnp.concatenate([col_hi, col_lo], axis=0)
    r, c = iota((2 * PATCH, PATCH), 0), iota((2 * PATCH, PATCH), 1) % 64
    horiz = jnp.where((r >= c) & (r < c + PATCH), 1.0, 0.0).astype(BF16)
    sums = [mm(parts[:, PATCH * p : PATCH * (p + 2)], horiz) for p in range(PCOL)]
    left = iota((40, PATCH), 1) < 64
    energies = [jnp.where(left, sums[2 * h][:40] + sums[2 * h][40:], sums[2 * h + 1][:40] + sums[2 * h + 1][40:]) for h in range(2)]
    ur, lane = iota((40, PATCH), 0), iota((40, PATCH), 1)
    for h in range(2):
        block = prod[:, pl.ds(PATCH * h, PATCH)].reshape(SPAN, JN, 8, PATCH)
        total = None
        for q in range(GROUP // 8):
            part = block[:, q]
            moved = pltpu.roll(part, PATCH - (GROUP - 1) + 8 * q, 2, stride=1, stride_axis=1)
            total = moved if total is None else total + moved
        numer = jnp.sum(total, axis=1)
        numer = jnp.concatenate([numer, jnp.zeros((40 - SPAN, PATCH), F32)], axis=0)
        scale = own_scale[0:1, PATCH * h : PATCH * (h + 1)] * lax.rsqrt(jnp.maximum(energies[h], FLOOR))
        score = numer * scale
        lines = []
        for k in range(5):
            line = score[8 * k : 8 * k + 8]
            line = pltpu.roll(line, 8 * k, 1) if k else line
            line = pltpu.roll(line, 0, 1, stride=16, stride_axis=0)
            lines.append(pltpu.roll(line, 0, 1, stride=17, stride_axis=0))
        both = jnp.concatenate(lines, axis=0)
        for q, moved in enumerate((both, pltpu.roll(both, 64, 1))):
            p = 2 * h + q
            for t in range(9):
                at = t * PATCH + lane
                pick = (at >= SPAN * ur) & (at < SPAN * ur + SPAN)
                line = jnp.sum(jnp.where(pick, moved, 0.0), axis=0, keepdims=True)
                count = min(PATCH, SPAN * SPAN - t * PATCH)
                out_ref[p : p + 1, t * PATCH : t * PATCH + count] = line[:, :count]


VMEM = pl.BlockSpec(memory_space=pltpu.VMEM)
RIM = 2 * BOX
INNER = PATCH - 2 * BOX
SLAB = RIM + 2 * BOX
FAR_SLAB = 40
FAR = 7
EARLY = 16
PARAMS = pltpu.CompilerParams(vmem_limit_bytes=48 << 20)
LONG = pl.CostEstimate(flops=1 << 33, bytes_accessed=1 << 20, transcendentals=0)
SHORT = pl.CostEstimate(flops=1, bytes_accessed=1, transcendentals=0)


def prepare_body(
    image_hbm, tissue_hbm, flags_hbm, core_ref, first_ref, second_ref, first_far_ref, second_far_ref, valid_ref,
    image, tissue, flags, sems,
):
    copies = [
        pltpu.make_async_copy(image_hbm, image, sems.at[0]),
        pltpu.make_async_copy(tissue_hbm, tissue, sems.at[1]),
        pltpu.make_async_copy(flags_hbm, flags, sems.at[2]),
    ]
    for copy in copies:
        copy.start()
    g = band()
    patch = iota((8, 64 * PCOL), 1) // 64
    copies[0].wait()
    x = image[...].astype(F32)
    scaled = standardized(x, INNER, g)
    copies[1].wait()
    copies[2].wait()
    marks = tissue[...].astype(F32)
    inner = (marks[BOX : PATCH - BOX] * scaled).astype(BF16)
    top, bottom = x[:RIM], x[PATCH - RIM :]
    top_marks, bottom_marks = marks[:BOX], marks[PATCH - BOX :]
    core_ref[:INNER] = inner
    core_ref[INNER:] = jnp.concatenate([top, bottom, top_marks, bottom_marks], axis=0).astype(BF16)
    inner = inner.astype(F32)
    upper = jnp.concatenate([inner[:BOX], top, top_marks], axis=0).astype(BF16)
    lower = jnp.concatenate([inner[INNER - BOX :], bottom, bottom_marks], axis=0).astype(BF16)
    valid = jnp.zeros((8, 64 * PCOL), jnp.int32)
    for p in range(PCOL):
        valid = jnp.where(patch == p, flags[p], valid)
    valid_ref[...] = valid.astype(F32)
    even = lax.axis_index("xy") % 2 == 0

    @pl.when(even)
    def _():
        first_ref[...] = upper
        second_ref[...] = lower
        first_far_ref[:SLAB] = upper
        second_far_ref[:SLAB] = lower

    @pl.when(jnp.logical_not(even))
    def _():
        first_ref[...] = lower
        second_ref[...] = upper
        first_far_ref[:SLAB] = lower
        second_far_ref[:SLAB] = upper


def completed(core, first, second):
    keep = jnp.where(lax.axis_index("xy") % 2 == 0, 1.0, 0.0).astype(F32)
    core, first, second = core.astype(F32), first.astype(F32), second.astype(F32)
    low = first * keep + second * (1.0 - keep)
    high = second * keep + first * (1.0 - keep)
    edges = core[INNER:]
    g = band()
    x = jnp.concatenate([low[BOX : BOX + RIM], edges[:RIM]], axis=0)
    tissue = jnp.concatenate([low[BOX + RIM :], edges[2 * RIM : 2 * RIM + BOX]], axis=0)
    above = normalized(x, tissue, g).astype(F32)
    x = jnp.concatenate([edges[RIM : 2 * RIM], high[BOX : BOX + RIM]], axis=0)
    tissue = jnp.concatenate([edges[2 * RIM + BOX :], high[BOX + RIM :]], axis=0)
    below = normalized(x, tissue, g).astype(F32)
    return jnp.concatenate([low[:BOX], above, core[:INNER], below, high[:BOX]], axis=0)


def complete_body(core_ref, first_ref, second_ref, early_first_ref, early_second_ref, out_ref):
    first = first_ref[...].astype(F32) + early_first_ref[...].astype(F32)
    second = second_ref[...].astype(F32) + early_second_ref[...].astype(F32)
    out_ref[...] = completed(core_ref[...], first, second).astype(BF16)


def choose_body(core_ref, first_ref, second_ref, out_ref):
    ready = (lax.axis_index("sec") == FAR + 1) & (lax.axis_index("xy") >= EARLY)

    @pl.when(ready)
    def _():
        out_ref[...] = completed(core_ref[...], first_ref[...], second_ref[...]).astype(BF16)

    @pl.when(jnp.logical_not(ready))
    def _():
        out_ref[...] = core_ref[...]


def shifted_body(own_ref, valid_ref, lhs_ref, own_scale_ref):
    shifted(own_ref[SEARCH : SEARCH + PATCH], valid_ref[...], lhs_ref, own_scale_ref)


def is_far():
    return lax.axis_index("sec") == FAR


def far_body(core_ref, first_ref, second_ref, own_scale_ref, out_ref):
    early = lax.axis_index("xy") < EARLY

    @pl.when(is_far() & early)
    def _():
        out_ref[...] = completed(core_ref[...], first_ref[:SLAB], second_ref[:SLAB]).astype(BF16)

    @pl.when(is_far() & jnp.logical_not(early))
    def _():
        out_ref[...] = core_ref[...]


def correlate_body(next_ref, far_ref, lhs_ref, own_scale_ref, out_ref, *scratch):
    b = jnp.where(is_far(), far_ref[...].astype(F32), next_ref[...].astype(F32))
    correlate(b, own_scale_ref[...], out_ref, lhs_ref, *scratch)


def odd_partner(i):
    return i - 1 if i % 2 == 0 else i + 1


def even_partner(i):
    return i + 1 if i % 2 == 0 else i - 1


def call(body, out_shape, operands, in_specs=None, scratch=(), cost=None):
    several = isinstance(out_shape, tuple)
    return pl.pallas_call(
        body,
        out_shape=out_shape,
        in_specs=in_specs or [VMEM] * len(operands),
        out_specs=(VMEM,) * len(out_shape) if several else VMEM,
        scratch_shapes=scratch,
        compiler_params=PARAMS,
        cost_estimate=cost,
    )(*operands)


def shards(image, mask, flags):
    image, mask, flags = image[0], mask[0], flags[0, 0]
    strips, sections = lax.axis_size("xy"), lax.axis_size("sec")
    odd = [(i, odd_partner(i)) for i in range(strips) if 0 <= odd_partner(i) < strips]
    even = [(i, even_partner(i)) for i in range(strips)]

    def rows(count):
        return jax.ShapeDtypeStruct((count, W), BF16)

    core, first, second, first_far, second_far, valid = call(
        prepare_body,
        (rows(PATCH + 2 * RIM), rows(SLAB), rows(SLAB), rows(FAR_SLAB), rows(FAR_SLAB), jax.ShapeDtypeStruct((8, 64 * PCOL), F32)),
        tuple(pltpu.with_memory_space_constraint(x, pltpu.HBM) for x in (image, mask, flags)),
        in_specs=[pl.BlockSpec(memory_space=pltpu.HBM)] * 3,
        scratch=[
            pltpu.VMEM((PATCH, W), BF16),
            pltpu.VMEM((PATCH, W), jnp.int32),
            pltpu.SMEM((PCOL,), jnp.int32),
            pltpu.SemaphoreType.DMA((3,)),
        ],
    )

    def swap(block, pairs, keep):
        route = [(s * strips + a, s * strips + b) for s in range(sections) for a, b in pairs if keep(s, a, b)]
        return lax.ppermute(block, ("sec", "xy"), route)

    def from_far(block, pairs):
        route = [((FAR + 1) * strips + a, FAR * strips + b) for a, b in pairs]
        return lax.ppermute(block, ("sec", "xy"), route)

    def ahead(s, a, b):
        return s == FAR + 1 and b >= EARLY

    def rest(s, a, b):
        return not ahead(s, a, b)

    early_first, early_second = swap(first, odd, ahead), swap(second, even, ahead)
    chosen = call(choose_body, rows(EXT), (core, early_first, early_second), cost=SHORT)
    core_far = from_far(chosen, [(i, i) for i in range(strips)])
    first_far = from_far(first_far, [(a, b) for a, b in odd if b < EARLY])
    second_far = from_far(second_far, [(a, b) for a, b in even if b < EARLY])
    first, second = swap(first, odd, rest), swap(second, even, rest)
    own = call(complete_body, rows(EXT), (core, first, second, early_first, early_second), cost=SHORT)
    following = lax.ppermute(own, "sec", [(s + 1, s) for s in range(sections - 1) if s != FAR])
    lhs, own_scale = call(
        shifted_body,
        (
            jax.ShapeDtypeStruct((SPAN * GROUP, JN * PCOL * EXT), BF16),
            jax.ShapeDtypeStruct((8, 64 * PCOL), F32),
        ),
        (own, valid),
        cost=SHORT,
    )
    far = call(far_body, rows(EXT), (core_far, first_far, second_far, own_scale), cost=LONG)
    scores = call(
        correlate_body,
        jax.ShapeDtypeStruct((PCOL, SPAN * SPAN), F32),
        (following, far, lhs, own_scale),
        scratch=[
            pltpu.VMEM((EXT, W + PATCH), F32),
            pltpu.VMEM((JN * PCOL * EXT, 64 * PCOL), BF16),
            pltpu.VMEM((SPAN * GROUP, 64 * PCOL), F32),
        ],
    )
    return scores[None, None]


def solution(mesh):
    placed = (P("sec", "xy", None), P("sec", "xy", None), P("sec", "xy", None))
    return jax.shard_map(
        shards, mesh=mesh, in_specs=placed, out_specs=P("sec", "xy", None, None), check_vma=False
    )
```

```python
import jax
import jax.numpy as jnp
from jax import lax
from jax.experimental import pallas as pl
from jax.experimental.pallas import tpu as pltpu
from jax.sharding import PartitionSpec as P

PATCH = 128
SEARCH = 16
BOX = 8
SPAN = 2 * SEARCH + 1
SIDE = 2 * BOX + 1
PCOL = 4
W = PCOL * PATCH
EXT = PATCH + 2 * SEARCH
GROUP = 32
JN = PATCH // GROUP
FLOOR = 0.25 * PATCH * PATCH
EPSILON = 1e-05
F32 = jnp.float32
BF16 = jnp.bfloat16


def iota(shape, dim):
    return lax.broadcasted_iota(jnp.int32, shape, dim)


def mm(a, b):
    return jnp.dot(a, b, preferred_element_type=F32)


def band():
    r, c = iota((W, W // 2), 0), iota((W, W // 2), 1)
    return jnp.where(jnp.abs(r - PATCH - c) <= BOX, 1.0, 0.0).astype(BF16)


def across(x, g):
    lo = mm(x[:, : 3 * PATCH], g[PATCH:])
    hi = mm(x[:, PATCH:], g[: 3 * PATCH])
    return jnp.concatenate([lo, hi], axis=1)


def down(s, rows):
    n = rows + SIDE - 1
    s2 = s[: n - 1] + s[1:]
    s4 = s2[: n - 3] + s2[2:]
    s8 = s4[: n - 7] + s4[4:]
    s16 = s8[: n - 15] + s8[8:]
    return s16[:rows] + s[SIDE - 1 : SIDE - 1 + rows]


def sums_across(x, g):
    sq = x * x
    sq_hi = sq.astype(BF16)
    sq_lo = (sq - sq_hi.astype(F32)).astype(BF16)
    return across(x.astype(BF16), g), across(sq_hi, g) + across(sq_lo, g)


def standardized(x, total, total_sq, rows):
    area = 1.0 / float(SIDE * SIDE)
    mean = down(total, rows) * area
    var = jnp.maximum(down(total_sq, rows) * area - mean * mean, 0.0)
    return (x[BOX : BOX + rows] - mean) * lax.rsqrt(var + EPSILON)


def shifted(a, valid, lhs, own_scale):
    r, c = iota((PATCH, PATCH), 0), iota((PATCH, PATCH), 1)
    flip = jnp.where((r // GROUP) * GROUP + (GROUP - 1 - r % GROUP) == c, 1.0, 0.0).astype(BF16)
    turned = [
        lax.dot_general(
            flip, a[:, PATCH * p : PATCH * (p + 1)], (((1,), (1,)), ((), ())), preferred_element_type=F32
        )
        for p in range(PCOL)
    ]
    lane = iota((PATCH, PATCH), 1)
    tiles = PCOL * EXT // PATCH
    for u in range(SPAN):
        parts = [None] * (tiles + 1)
        for p in range(PCOL):
            t, o = divmod(EXT * p + u, PATCH)
            moved = pltpu.roll(turned[p], o, 1) if o else turned[p]
            for tile, keep in ((t, lane >= o), (t + 1, lane < o)):
                if tile == t + 1 and o == 0:
                    continue
                base = parts[tile]
                parts[tile] = jnp.where(keep, moved, 0.0 if base is None else base)
        for tile in range(tiles):
            val = parts[tile].astype(BF16)
            for j in range(JN):
                lhs[pl.ds(u * GROUP, GROUP), pl.ds((j * tiles + tile) * PATCH, PATCH)] = val[GROUP * j : GROUP * (j + 1)]
    xr, xc = iota((W, 64 * PCOL), 0), iota((W, 64 * PCOL), 1)
    af = a.astype(F32)
    own = jnp.sum(af * af, axis=0, keepdims=True)
    own_hi = own.astype(BF16)
    own_lo = (own - own_hi.astype(F32)).astype(BF16)
    same = jnp.where(xr // PATCH == xc // 64, 1.0, 0.0).astype(BF16)
    own8 = jnp.concatenate([own_hi, own_lo, jnp.zeros((14, W), BF16)], axis=0)
    own_sum = mm(own8, same)
    energy_own = own_sum[0:1] + own_sum[1:2]
    own_scale[...] = valid * lax.rsqrt(jnp.maximum(energy_own, FLOOR))


def correlate(b, own_scale, out_ref, lhs, wide, wgt, prod):
    wide[:, :PATCH] = jnp.zeros((EXT, PATCH), F32)
    wide[:, W:] = jnp.zeros((EXT, PATCH), F32)
    wide[:, SEARCH : SEARCH + W] = b
    lane = iota((EXT, PATCH), 1)
    for p in range(PCOL):
        h, q = divmod(p, 2)
        one, two = wide[:, PATCH * p : PATCH * (p + 1)], wide[:, PATCH * (p + 1) : PATCH * (p + 2)]
        for j in range(JN):
            turn = (64 * q - GROUP * j) % PATCH
            piece = pltpu.roll(one, turn, 1) if turn else one
            if j == JN - 1:
                piece = jnp.where(lane < 64 * q + GROUP, piece, pltpu.roll(two, turn, 1) if turn else two)
            rows = pl.ds((j * PCOL + p) * EXT, EXT)
            keep = lane < 64 if q == 0 else lane >= 64
            wgt[rows, pl.ds(PATCH * h, PATCH)] = jnp.where(keep, piece, 0.0).astype(BF16)
            wgt[rows, pl.ds(PATCH * (1 - h), PATCH)] = jnp.zeros((EXT, PATCH), BF16)
    prod[...] = mm(lhs[...], wgt[...])
    sq = wide[...] * wide[...]
    sq_hi = sq.astype(BF16)
    sq_lo = (sq - sq_hi.astype(F32)).astype(BF16)
    r, c = iota((40, EXT), 0), iota((40, EXT), 1)
    vert = jnp.where((c >= r) & (c < r + PATCH), 1.0, 0.0).astype(BF16)
    col = mm(vert, sq_hi) + mm(vert, sq_lo)
    col_hi = col.astype(BF16)
    col_lo = (col - col_hi.astype(F32)).astype(BF16)
    parts = jnp.concatenate([col_hi, col_lo], axis=0)
    r, c = iota((2 * PATCH, PATCH), 0), iota((2 * PATCH, PATCH), 1) % 64
    horiz = jnp.where((r >= c) & (r < c + PATCH), 1.0, 0.0).astype(BF16)
    sums = [mm(parts[:, PATCH * p : PATCH * (p + 2)], horiz) for p in range(PCOL)]
    left = iota((40, PATCH), 1) < 64
    energies = [jnp.where(left, sums[2 * h][:40] + sums[2 * h][40:], sums[2 * h + 1][:40] + sums[2 * h + 1][40:]) for h in range(2)]
    ur, lane = iota((40, PATCH), 0), iota((40, PATCH), 1)
    for h in range(2):
        block = prod[:, pl.ds(PATCH * h, PATCH)].reshape(SPAN, JN, 8, PATCH)
        total = None
        for q in range(GROUP // 8):
            part = block[:, q]
            moved = pltpu.roll(part, PATCH - (GROUP - 1) + 8 * q, 2, stride=1, stride_axis=1)
            total = moved if total is None else total + moved
        numer = jnp.sum(total, axis=1)
        numer = jnp.concatenate([numer, jnp.zeros((40 - SPAN, PATCH), F32)], axis=0)
        scale = own_scale[0:1, PATCH * h : PATCH * (h + 1)] * lax.rsqrt(jnp.maximum(energies[h], FLOOR))
        score = numer * scale
        lines = []
        for k in range(5):
            line = score[8 * k : 8 * k + 8]
            line = pltpu.roll(line, 8 * k, 1) if k else line
            line = pltpu.roll(line, 0, 1, stride=16, stride_axis=0)
            lines.append(pltpu.roll(line, 0, 1, stride=17, stride_axis=0))
        both = jnp.concatenate(lines, axis=0)
        for q, moved in enumerate((both, pltpu.roll(both, 64, 1))):
            p = 2 * h + q
            for t in range(9):
                at = t * PATCH + lane
                pick = (at >= SPAN * ur) & (at < SPAN * ur + SPAN)
                line = jnp.sum(jnp.where(pick, moved, 0.0), axis=0, keepdims=True)
                count = min(PATCH, SPAN * SPAN - t * PATCH)
                out_ref[p : p + 1, t * PATCH : t * PATCH + count] = line[:, :count]


VMEM = pl.BlockSpec(memory_space=pltpu.VMEM)
RIM = 2 * BOX
INNER = PATCH - 2 * BOX
SLAB = RIM + 2 * BOX
FAR_SLAB = 40
FAR = 7
EARLY = 20
PARAMS = pltpu.CompilerParams(vmem_limit_bytes=48 << 20)
LONG = pl.CostEstimate(flops=1 << 33, bytes_accessed=1 << 20, transcendentals=0)
SHORT = pl.CostEstimate(flops=1, bytes_accessed=1, transcendentals=0)


def prepare_body(
    image_hbm, tissue_hbm, flags_hbm, core_ref, first_ref, second_ref, first_far_ref, second_far_ref, valid_ref, band_ref,
    image, tissue, flags, sems,
):
    copies = [
        pltpu.make_async_copy(image_hbm, image, sems.at[0]),
        pltpu.make_async_copy(tissue_hbm, tissue, sems.at[1]),
        pltpu.make_async_copy(flags_hbm, flags, sems.at[2]),
    ]
    for copy in copies:
        copy.start()
    g = band()
    band_ref[...] = g
    patch = iota((8, 64 * PCOL), 1) // 64
    copies[0].wait()
    x = image[...].astype(F32)
    scaled = standardized(x, *sums_across(x, g), INNER)
    copies[1].wait()
    copies[2].wait()
    marks = tissue[...].astype(F32)
    inner = (marks[BOX : PATCH - BOX] * scaled).astype(BF16)
    top, bottom = x[:RIM], x[PATCH - RIM :]
    top_marks, bottom_marks = marks[:BOX], marks[PATCH - BOX :]
    core_ref[:INNER] = inner
    core_ref[INNER:] = jnp.concatenate([top, bottom, top_marks, bottom_marks], axis=0).astype(BF16)
    inner = inner.astype(F32)
    upper = jnp.concatenate([inner[:BOX], top, top_marks], axis=0).astype(BF16)
    lower = jnp.concatenate([inner[INNER - BOX :], bottom, bottom_marks], axis=0).astype(BF16)
    valid = jnp.zeros((8, 64 * PCOL), jnp.int32)
    for p in range(PCOL):
        valid = jnp.where(patch == p, flags[p], valid)
    valid_ref[...] = valid.astype(F32)
    even = lax.axis_index("xy") % 2 == 0

    @pl.when(even)
    def _():
        first_ref[...] = upper
        second_ref[...] = lower
        first_far_ref[:SLAB] = upper
        second_far_ref[:SLAB] = lower

    @pl.when(jnp.logical_not(even))
    def _():
        first_ref[...] = lower
        second_ref[...] = upper
        first_far_ref[:SLAB] = lower
        second_far_ref[:SLAB] = upper


def completed(core, first, second, g):
    keep = jnp.where(lax.axis_index("xy") % 2 == 0, 1.0, 0.0).astype(F32)
    core, first, second = core.astype(F32), first.astype(F32), second.astype(F32)
    low = first * keep + second * (1.0 - keep)
    high = second * keep + first * (1.0 - keep)
    edges = core[INNER:]
    x = jnp.concatenate([low[BOX : BOX + RIM], edges[: 2 * RIM], high[BOX : BOX + RIM]], axis=0)
    total, total_sq = sums_across(x, g)
    marks = edges[2 * RIM :]
    n = 2 * RIM
    above = jnp.concatenate([low[BOX + RIM :], marks[:BOX]], axis=0) * standardized(x[:n], total[:n], total_sq[:n], RIM)
    below = jnp.concatenate([marks[BOX:], high[BOX + RIM :]], axis=0) * standardized(x[n:], total[n:], total_sq[n:], RIM)
    return jnp.concatenate([low[:BOX], above, core[:INNER], below, high[:BOX]], axis=0)


def complete_body(core_ref, first_ref, second_ref, early_first_ref, early_second_ref, band_ref, out_ref):
    first = first_ref[...].astype(F32) + early_first_ref[...].astype(F32)
    second = second_ref[...].astype(F32) + early_second_ref[...].astype(F32)
    out_ref[...] = completed(core_ref[...], first, second, band_ref[...]).astype(BF16)


def choose_body(core_ref, first_ref, second_ref, band_ref, out_ref):
    ready = (lax.axis_index("sec") == FAR + 1) & (lax.axis_index("xy") >= EARLY)

    @pl.when(ready)
    def _():
        out_ref[...] = completed(core_ref[...], first_ref[...], second_ref[...], band_ref[...]).astype(BF16)

    @pl.when(jnp.logical_not(ready))
    def _():
        out_ref[...] = core_ref[...]


def shifted_body(own_ref, valid_ref, lhs_ref, own_scale_ref):
    shifted(own_ref[SEARCH : SEARCH + PATCH], valid_ref[...], lhs_ref, own_scale_ref)


def is_far():
    return lax.axis_index("sec") == FAR


def far_body(core_ref, first_ref, second_ref, own_scale_ref, band_ref, out_ref):
    early = lax.axis_index("xy") < EARLY

    @pl.when(is_far() & early)
    def _():
        out_ref[...] = completed(core_ref[...], first_ref[:SLAB], second_ref[:SLAB], band_ref[...]).astype(BF16)

    @pl.when(is_far() & jnp.logical_not(early))
    def _():
        out_ref[...] = core_ref[...]


def correlate_body(next_ref, far_ref, lhs_ref, own_scale_ref, out_ref, *scratch):
    b = jnp.where(is_far(), far_ref[...].astype(F32), next_ref[...].astype(F32))
    correlate(b, own_scale_ref[...], out_ref, lhs_ref, *scratch)


def odd_partner(i):
    return i - 1 if i % 2 == 0 else i + 1


def even_partner(i):
    return i + 1 if i % 2 == 0 else i - 1


def call(body, out_shape, operands, in_specs=None, scratch=(), cost=None):
    several = isinstance(out_shape, tuple)
    return pl.pallas_call(
        body,
        out_shape=out_shape,
        in_specs=in_specs or [VMEM] * len(operands),
        out_specs=(VMEM,) * len(out_shape) if several else VMEM,
        scratch_shapes=scratch,
        compiler_params=PARAMS,
        cost_estimate=cost,
    )(*operands)


def shards(image, mask, flags):
    image, mask, flags = image[0], mask[0], flags[0, 0]
    strips, sections = lax.axis_size("xy"), lax.axis_size("sec")
    odd = [(i, odd_partner(i)) for i in range(strips) if 0 <= odd_partner(i) < strips]
    even = [(i, even_partner(i)) for i in range(strips)]

    def rows(count):
        return jax.ShapeDtypeStruct((count, W), BF16)

    core, first, second, first_far, second_far, valid, bands = call(
        prepare_body,
        (rows(PATCH + 2 * RIM), rows(SLAB), rows(SLAB), rows(FAR_SLAB), rows(FAR_SLAB), jax.ShapeDtypeStruct((8, 64 * PCOL), F32), jax.ShapeDtypeStruct((W, W // 2), BF16)),
        tuple(pltpu.with_memory_space_constraint(x, pltpu.HBM) for x in (image, mask, flags)),
        in_specs=[pl.BlockSpec(memory_space=pltpu.HBM)] * 3,
        scratch=[
            pltpu.VMEM((PATCH, W), BF16),
            pltpu.VMEM((PATCH, W), jnp.int32),
            pltpu.SMEM((PCOL,), jnp.int32),
            pltpu.SemaphoreType.DMA((3,)),
        ],
    )

    def swap(block, pairs, keep):
        route = [(s * strips + a, s * strips + b) for s in range(sections) for a, b in pairs if keep(s, a, b)]
        return lax.ppermute(block, ("sec", "xy"), route)

    def from_far(block, pairs):
        route = [((FAR + 1) * strips + a, FAR * strips + b) for a, b in pairs]
        return lax.ppermute(block, ("sec", "xy"), route)

    def ahead(s, a, b):
        return s == FAR + 1 and b >= EARLY

    def rest(s, a, b):
        return not ahead(s, a, b)

    early_first, early_second = swap(first, odd, ahead), swap(second, even, ahead)
    chosen = call(choose_body, rows(EXT), (core, early_first, early_second, bands), cost=SHORT)
    core_far = from_far(chosen, [(i, i) for i in range(strips)])
    first_far = from_far(first_far, [(a, b) for a, b in odd if b < EARLY])
    second_far = from_far(second_far, [(a, b) for a, b in even if b < EARLY])
    first, second = swap(first, odd, rest), swap(second, even, rest)
    own = call(complete_body, rows(EXT), (core, first, second, early_first, early_second, bands), cost=SHORT)
    following = lax.ppermute(own, "sec", [(s + 1, s) for s in range(sections - 1) if s != FAR])
    lhs, own_scale = call(
        shifted_body,
        (
            jax.ShapeDtypeStruct((SPAN * GROUP, JN * PCOL * EXT), BF16),
            jax.ShapeDtypeStruct((8, 64 * PCOL), F32),
        ),
        (own, valid),
        cost=SHORT,
    )
    far = call(far_body, rows(EXT), (core_far, first_far, second_far, own_scale, bands), cost=LONG)
    scores = call(
        correlate_body,
        jax.ShapeDtypeStruct((PCOL, SPAN * SPAN), F32),
        (following, far, lhs, own_scale),
        scratch=[
            pltpu.VMEM((EXT, W + PATCH), F32),
            pltpu.VMEM((JN * PCOL * EXT, 64 * PCOL), BF16),
            pltpu.VMEM((SPAN * GROUP, 64 * PCOL), F32),
        ],
    )
    return scores[None, None]


def solution(mesh):
    placed = (P("sec", "xy", None), P("sec", "xy", None), P("sec", "xy", None))
    return jax.shard_map(
        shards, mesh=mesh, in_specs=placed, out_specs=P("sec", "xy", None, None), check_vma=False
    )
```
